512 devices in a mesh: ctx: 64 (over y_lo, z, core), head: 8 (over x, y_hi).
Axes of the slice: x: 4, y: 4 (y_hi: 2, y_lo: 2; y = y_hi * 2 + y_lo), z: 16, core: 2. Of those that a mesh axis runs over, the one named last changes fastest.
Arguments:
- queries: bfloat16 [16384, 8192], P(('ctx', 'head')), may hold values from -6 to 6
- keys: bfloat16 [16384, 1024], P(('ctx', 'head')), may hold values from -6 to 6
- values: bfloat16 [16384, 1024], P(('ctx', 'head')), may hold values from -6 to 6
- output_gradient: bfloat16 [16384, 8192], P(('ctx', 'head')), may hold values from -6 to 6
- doc_lengths: int32 [32], replicated, may hold values from 1 to 1024, 16384 in all
Outputs:
- attention: bfloat16 [16384, 8192], P(('ctx', 'head'))
- grad_queries: bfloat16 [16384, 8192], P(('ctx', 'head'))
- key_gradient: bfloat16 [16384, 1024], P(('ctx', 'head'))
- value_gradient: bfloat16 [16384, 1024], P(('ctx', 'head'))
The draws below stay inside these ranges and needn't reach their ends.
Inputs may be any that keep to these rules, and one draw needn't show every extreme that they name: `doc_lengths`: document lengths sum to 16384; the longest has exactly 1024 tokens.
All inputs are finite; a program needn't handle non-finite values.
Results may differ from the reference program's by a relative error of at most 0.03.
Values may be sent and summed in bfloat16 or wider, within the bound.
A program may use at most 64 MiB of HBM per device.

```python
import math
import jax
import jax.numpy as jnp
import numpy as np
from jax import lax

HEAD_WIDTH = 128
QUERY_HEADS = 64
KEY_VALUE_HEADS = 8
TOK_SHARD = 256
SPAN = 4
DOCS = 32
PACKED_TOKENS = 16384
MOST = 1024


def draw_queries(key, part):
    key = jax.random.fold_in(key, 1)
    heads_per_group = QUERY_HEADS // KEY_VALUE_HEADS
    base_offset = jnp.clip(jax.random.normal(key, (PACKED_TOKENS, KEY_VALUE_HEADS, heads_per_group, HEAD_WIDTH), jnp.float32), -6.0, 6.0)
    return base_offset.reshape(PACKED_TOKENS, QUERY_HEADS * HEAD_WIDTH).astype(jnp.bfloat16)


def draw_keys(key, part):
    key = jax.random.fold_in(key, 2)
    base_offset = jnp.clip(jax.random.normal(key, (PACKED_TOKENS, KEY_VALUE_HEADS, HEAD_WIDTH), jnp.float32), -6.0, 6.0)
    return base_offset.reshape(PACKED_TOKENS, KEY_VALUE_HEADS * HEAD_WIDTH).astype(jnp.bfloat16)


def level_of(stream_key, dims, cuts, least, largest):
    factor_of, own = 1.0, jax.random.fold_in(stream_key, 6)
    for axis_at, shards_of in cuts:
        heights = jnp.exp(jax.random.uniform(jax.random.fold_in(own, axis_at), (shards_of,), jnp.float32, least / len(cuts), largest / len(cuts)))
        factor_of = factor_of * jnp.repeat(heights, dims[axis_at] // shards_of).reshape([-1 if axis == axis_at else 1 for axis in range(len(dims))])
    return factor_of


def split_up(amount, total, bound, slope):
    portions = [(1 << 20) // math.isqrt(grade ** slope) + 1 for grade in range(2, amount + 1)]
    surplus, holding = total - bound - (amount - 1), [1] * (amount - 1)
    while surplus > 0:
        candidates = [i for i in range(amount - 1) if holding[i] < bound]
        mass, left = sum([portions[i] for i in candidates]), surplus
        for i in candidates:
            extra = min(bound - holding[i], max(1, left * portions[i] // mass), surplus)
            holding[i] = holding[i] + extra
            surplus = surplus - extra
    return np.array([bound] + holding)


def ragged(own_key, amount, total, most, lean):
    if amount == 2:
        one = jax.random.randint(own_key, (), max(1, total - most), min(most, total - 1) + 1)
        return jnp.stack([one, total - one])
    sizes = jnp.asarray(split_up(amount, total, most, lean), jnp.int32)
    twos = (amount - 1) // 2
    source_of, taker = sizes[1:1 + 2 * twos:2], sizes[2:2 + 2 * twos:2]
    room = jnp.minimum(source_of - 1, most - taker)
    shifted = jax.random.randint(jax.random.fold_in(own_key, 1), (twos,), 0, 1 << 20) % (room + 1)
    sizes = sizes.at[1:1 + 2 * twos:2].set(source_of - shifted).at[2:2 + 2 * twos:2].set(taker + shifted)
    return sizes[jax.random.permutation(jax.random.fold_in(own_key, 2), amount)]


def centred(rng, shape, scale, reach, split=(), held_as=jnp.bfloat16):
    drawn = jax.random.normal(rng, shape, jnp.float32) * scale
    if len(split) > 0:
        drawn = level_of(rng, shape, split, -0.22, 0.18) * drawn
    return jnp.clip(drawn, min=-reach, max=reach).astype(held_as)


def setup_inputs(seed: int = 0) -> dict:
    seeds = jax.random.split(jax.random.key(seed), 6)
    queries = draw_queries(jax.random.fold_in(seeds[5], 71), 0)
    keys = draw_keys(jax.random.fold_in(seeds[5], 71), 0)
    values = centred(seeds[2], (PACKED_TOKENS, KEY_VALUE_HEADS * HEAD_WIDTH), 1.0, 6.0, ((0, 512),))
    output_gradient = centred(seeds[3], (PACKED_TOKENS, QUERY_HEADS * HEAD_WIDTH), 1.0, 6.0, ((0, 512),))
    doc_lengths = ragged(seeds[4], DOCS, PACKED_TOKENS, MOST, 2).astype(jnp.int32)
    return dict(queries=queries, keys=keys, values=values, output_gradient=output_gradient, doc_lengths=doc_lengths)


def reference(queries, keys, values, output_gradient, doc_lengths):
    heads_per_group = QUERY_HEADS // KEY_VALUE_HEADS
    score_scale = 1.0 / math.sqrt(HEAD_WIDTH)
    row_span = SPAN * TOK_SHARD
    window = row_span + TOK_SHARD
    doc_ends = jnp.cumsum(doc_lengths).astype(jnp.int32)
    query_whole = queries.reshape(PACKED_TOKENS, KEY_VALUE_HEADS, heads_per_group, HEAD_WIDTH)
    gradient_whole = output_gradient.reshape(PACKED_TOKENS, KEY_VALUE_HEADS, heads_per_group, HEAD_WIDTH)

    def padded(block_size):
        return jnp.concatenate([jnp.zeros((row_span, KEY_VALUE_HEADS, HEAD_WIDTH), block_size.dtype), block_size.reshape(PACKED_TOKENS, KEY_VALUE_HEADS, HEAD_WIDTH)], axis=0)
    key_all = padded(keys)
    value_all = padded(values)

    def document_ids(start, count):
        positions = start + jnp.arange(count, dtype=jnp.int32)
        ids = lax.optimization_barrier(jnp.sum((doc_ends[None, :] <= positions[:, None]).astype(jnp.int32), axis=1))
        return (ids, positions)

    def one_block(carry, index):
        key_gathered, value_gathered = carry
        start = (index * TOK_SHARD).astype(jnp.int32)
        query_block = lax.dynamic_slice_in_dim(query_whole, start, TOK_SHARD, 0).astype(jnp.float32)
        grad_block = lax.dynamic_slice_in_dim(gradient_whole, start, TOK_SHARD, 0).astype(jnp.float32)
        key_block = lax.dynamic_slice_in_dim(key_all, start, window, 0).astype(jnp.float32)
        value_block = lax.dynamic_slice_in_dim(value_all, start, window, 0).astype(jnp.float32)
        query_ids, query_pos = document_ids(start, TOK_SHARD)
        key_ids, key_pos = document_ids(start - row_span, window)
        allowed = (query_ids[:, None] == key_ids[None, :]) & (key_pos[None, :] >= 0) & (key_pos[None, :] <= query_pos[:, None])
        raw = jnp.einsum('sagd,tad->agst', query_block, key_block) * score_scale
        masked = jnp.where(allowed, raw, -jnp.inf)
        top = lax.optimization_barrier(jnp.max(masked, axis=-1))
        log_total = top + jnp.log(lax.optimization_barrier(jnp.sum(jnp.exp(masked - top[..., None]), axis=-1)))
        probs = jnp.exp(masked - log_total[..., None])
        weights = lax.optimization_barrier(probs.astype(jnp.bfloat16)).astype(jnp.float32)
        attention_block = jnp.einsum('agst,tad->sagd', weights, value_block).astype(jnp.bfloat16)
        attention_wide = lax.optimization_barrier(attention_block).astype(jnp.float32)
        delta = jnp.transpose(lax.optimization_barrier(jnp.sum(grad_block * attention_wide, axis=-1)), (1, 2, 0))
        prob_grad = jnp.einsum('sagd,tad->agst', grad_block, value_block)
        dscore = (probs * (prob_grad - delta[..., None]) * score_scale).astype(jnp.bfloat16)
        dscore = lax.optimization_barrier(dscore).astype(jnp.float32)
        query_grad = jnp.einsum('agst,tad->sagd', dscore, key_block).astype(jnp.bfloat16)
        key_part = jnp.einsum('agst,sagd->tad', dscore, query_block)
        value_part = jnp.einsum('agst,sagd->tad', weights, grad_block)
        key_gathered = lax.dynamic_update_slice_in_dim(key_gathered, lax.dynamic_slice_in_dim(key_gathered, start, window, 0) + key_part, start, 0)
        value_gathered = lax.dynamic_update_slice_in_dim(value_gathered, lax.dynamic_slice_in_dim(value_gathered, start, window, 0) + value_part, start, 0)
        return ((key_gathered, value_gathered), (attention_block, query_grad))
    start_gathered = jnp.zeros((PACKED_TOKENS + row_span, KEY_VALUE_HEADS, HEAD_WIDTH), jnp.float32)
    (key_gathered, value_gathered), (attention_blocks, query_grads) = lax.scan(one_block, (start_gathered, start_gathered), jnp.arange(PACKED_TOKENS // TOK_SHARD, dtype=jnp.int32))
    attention = attention_blocks.reshape(PACKED_TOKENS, QUERY_HEADS * HEAD_WIDTH)
    grad_queries = query_grads.reshape(PACKED_TOKENS, QUERY_HEADS * HEAD_WIDTH)
    key_gradient = key_gathered[row_span:].reshape(PACKED_TOKENS, KEY_VALUE_HEADS * HEAD_WIDTH).astype(jnp.bfloat16)
    value_gradient = value_gathered[row_span:].reshape(PACKED_TOKENS, KEY_VALUE_HEADS * HEAD_WIDTH).astype(jnp.bfloat16)
    return (attention, grad_queries, key_gradient, value_gradient)
```

```python
import math

import jax
import jax.numpy as jnp
from jax import lax
from jax.experimental import pallas as pl
from jax.experimental.pallas import tpu as pltpu
from jax.sharding import PartitionSpec as P

HEAD_WIDTH = 128
QUERY_HEADS = 64
KEY_VALUE_HEADS = 8
DOCS = 32
SHARDS = 64
GROUPS = 8
PER_GROUP = 8
PIECE = 32
SHARD = 256
WINDOW = 1280
REACH = 1152
CHUNK = 384
ROWS = PER_GROUP * PIECE
COLS = PER_GROUP * HEAD_WIDTH
SCALE = 1.0 / math.sqrt(HEAD_WIDTH)
SCALE2 = SCALE * math.log2(math.e)
MESH = pl.DeviceIdType.MESH
F32 = jnp.float32
BF16 = jnp.bfloat16


def dot_nn(a, b):
    return lax.dot_general(a, b, (((1,), (0,)), ((), ())), preferred_element_type=F32)


def dot_nt(a, b):
    return lax.dot_general(a, b, (((1,), (1,)), ((), ())), preferred_element_type=F32)


def stack_heads(piece):
    return jnp.concatenate(
        [piece[:, g * HEAD_WIDTH : (g + 1) * HEAD_WIDTH] for g in range(PER_GROUP)], axis=0
    )


def store_heads(ref, piece, rows):
    for g in range(PER_GROUP):
        ref[piece, :, g * HEAD_WIDTH : (g + 1) * HEAD_WIDTH] = rows[g * PIECE : (g + 1) * PIECE]


def attend(piece, shard_start, lens, qbuf, gbuf, kv, kv_t, obuf, dqbuf, acc, s_buf, dp_buf, p_buf):
    off = pl.multiple_of((piece // 4) * 128, 128)
    q_t = stack_heads(qbuf[piece]).T
    g_t = stack_heads(gbuf[piece]).T
    pos = shard_start + piece * PIECE + lax.rem(lax.broadcasted_iota(jnp.int32, (1, ROWS), 1), PIECE)
    start = jnp.zeros((1, ROWS), jnp.int32)
    end = jnp.int32(0)
    for n in range(DOCS):
        end = end + lens[n]
        start = jnp.where(pos >= end, end, start)
    first = shard_start - (WINDOW - SHARD) + off
    low = start - first
    high = pos - first
    top = jnp.full((1, ROWS), -jnp.inf, F32)
    for r in range(0, REACH, CHUNK):
        s = dot_nn(kv[0, pl.ds(off + r, CHUNK), :], q_t)
        at = lax.broadcasted_iota(jnp.int32, (CHUNK, ROWS), 0) + r
        allowed = at >= low
        if r + CHUNK > REACH - 128:
            allowed = allowed & (at <= high)
        s = jnp.where(allowed, s, -1e30)
        s_buf[r : r + CHUNK, :] = s
        top = jnp.maximum(top, jnp.max(s, axis=0, keepdims=True))
        dp_buf[r : r + CHUNK, :] = dot_nn(kv[1, pl.ds(off + r, CHUNK), :], g_t)
    total = jnp.zeros((1, ROWS), F32)
    o_t = jnp.zeros((HEAD_WIDTH, ROWS), F32)
    for r in range(0, REACH, CHUNK):
        p = jnp.exp2((s_buf[r : r + CHUNK, :] - top) * SCALE2)
        total = total + jnp.sum(p, axis=0, keepdims=True)
        p_b = p.astype(BF16)
        s_buf[r : r + CHUNK, :] = p
        p_buf[r : r + CHUNK, :] = p_b
        o_t = o_t + dot_nn(kv_t[1, :, pl.ds(pl.multiple_of(off + r, 128), CHUNK)], p_b)
    inv = 1.0 / total
    g_f = g_t.astype(F32)
    o_b = (o_t * inv).astype(BF16)
    delta = jnp.sum(g_f * o_b.astype(F32), axis=0, keepdims=True)
    g_n = (g_f * inv).astype(BF16)
    q_n = (q_t.astype(F32) * inv).astype(BF16)
    store_heads(obuf, piece, o_b.T)
    dq_t = jnp.zeros((HEAD_WIDTH, ROWS), F32)
    for r in range(0, REACH, CHUNK):
        ds = (s_buf[r : r + CHUNK, :] * (dp_buf[r : r + CHUNK, :] - delta)).astype(BF16)
        dq_t = dq_t + dot_nn(kv_t[0, :, pl.ds(pl.multiple_of(off + r, 128), CHUNK)], ds)
        acc[0, pl.ds(off + r, CHUNK), :] += dot_nt(ds, q_n)
        acc[1, pl.ds(off + r, CHUNK), :] += dot_nt(p_buf[r : r + CHUNK, :], g_n)
    store_heads(dqbuf, piece, (dq_t * (inv * SCALE)).astype(BF16).T)


def kernel(
    q_in, k_in, v_in, g_in, lens,
    o_out, dq_out, dk_out, dv_out,
    qbuf, gbuf, kv, kv_t, obuf, dqbuf, acc, s_buf, dp_buf, p_buf,
    swap_out, swap_in, far_out, far_in, last,
    q_sem, g_sem, kv_sem, fwd_sem, swap_sem, back_sem, far_sem,
    o_sem, dq_sem, dk_sem, dv_sem, send_sem,
):
    c = lax.axis_index("ctx")
    me = lax.axis_index("head")
    core = lax.rem(c, 2)
    other = (c + 1 - 2 * core, me)
    along = {d: (lax.rem(c + d + SHARDS, SHARDS), me) for d in (2, 4, -2, -4)}
    peers = [lax.rem(me + i, GROUPS) for i in range(GROUPS)]
    takers = [lax.rem(me - i + GROUPS, GROUPS) for i in range(GROUPS)]
    own = slice(WINDOW - SHARD, WINDOW)

    def columns(h, width):
        return pl.ds(pl.multiple_of(h * width, width), width)

    def rows_of(h):
        return pl.ds(pl.multiple_of(WINDOW - SHARD + h * PIECE, PIECE), PIECE)

    local = [
        pltpu.make_async_copy(k_in.at[:, columns(me, HEAD_WIDTH)], kv.at[0, rows_of(me)], kv_sem),
        pltpu.make_async_copy(v_in.at[:, columns(me, HEAD_WIDTH)], kv.at[1, rows_of(me)], kv_sem),
        pltpu.make_async_copy(q_in.at[:, columns(me, COLS)], qbuf.at[me], q_sem.at[0]),
        pltpu.make_async_copy(g_in.at[:, columns(me, COLS)], gbuf.at[me], g_sem.at[0]),
    ]
    for copy in local:
        copy.start()

    barrier = pltpu.get_barrier_semaphore()
    partners = [(c, peers[i]) for i in range(1, GROUPS)] + [other] + list(along.values())
    for partner in partners:
        pl.semaphore_signal(barrier, inc=1, device_id=partner, device_id_type=MESH)
    pl.semaphore_wait(barrier, len(partners))

    def send(src, dst, sent, landed, to):
        pltpu.make_async_remote_copy(
            src_ref=src, dst_ref=dst, send_sem=sent, recv_sem=landed, device_id=to, device_id_type=MESH
        ).start()

    def landed(ref, sem):
        pltpu.make_async_copy(ref, ref, sem).wait()

    for i in range(1, GROUPS):
        to = (c, takers[i])
        send(k_in.at[:, columns(takers[i], HEAD_WIDTH)], kv.at[0, rows_of(me)], send_sem.at[0], kv_sem, to)
        send(v_in.at[:, columns(takers[i], HEAD_WIDTH)], kv.at[1, rows_of(me)], send_sem.at[0], kv_sem, to)
    for i in range(1, GROUPS):
        to = (c, takers[i])
        send(q_in.at[:, columns(takers[i], COLS)], qbuf.at[me], send_sem.at[1], q_sem.at[i], to)
        send(g_in.at[:, columns(takers[i], COLS)], gbuf.at[me], send_sem.at[2], g_sem.at[i], to)

    acc[...] = jnp.zeros_like(acc)

    def back(distance):
        return pl.ds(pl.multiple_of((4 - distance) * SHARD, SHARD), SHARD)

    landed(kv.at[:, own], kv_sem)
    send(kv.at[:, own], kv.at[:, back(2)], send_sem.at[3], fwd_sem.at[0], along[2])
    send(kv.at[:, own], kv.at[:, back(4)], send_sem.at[4], fwd_sem.at[1], along[4])
    landed(kv.at[:, back(2)], fwd_sem.at[0])
    send(kv.at[:, back(2 * core)], kv.at[:, back(1)], send_sem.at[5], swap_sem.at[0], other)
    landed(kv.at[:, back(4)], fwd_sem.at[1])
    send(kv.at[:, back(2 * core + 2)], kv.at[:, back(3)], send_sem.at[6], swap_sem.at[1], other)
    landed(kv.at[:, back(1)], swap_sem.at[0])
    landed(kv.at[:, back(3)], swap_sem.at[1])
    kv_t[0] = kv[0].T
    kv_t[1] = kv[1].T

    def step(i, carry):
        peer = lax.rem(me + i, GROUPS)
        landed(qbuf.at[peer], q_sem.at[i])
        landed(gbuf.at[peer], g_sem.at[i])
        attend(peer, c * SHARD, lens, qbuf, gbuf, kv, kv_t, obuf, dqbuf, acc, s_buf, dp_buf, p_buf)

        @pl.when(i == 0)
        def _():
            pltpu.make_async_copy(obuf.at[me], o_out.at[:, columns(me, COLS)], o_sem).start()
            pltpu.make_async_copy(dqbuf.at[me], dq_out.at[:, columns(me, COLS)], dq_sem).start()

        @pl.when(i > 0)
        def _():
            send(obuf.at[peer], o_out.at[:, columns(me, COLS)], send_sem.at[7], o_sem, (c, peer))
            send(dqbuf.at[peer], dq_out.at[:, columns(me, COLS)], send_sem.at[8], dq_sem, (c, peer))

        return carry

    lax.fori_loop(0, GROUPS, step, 0)

    def part(distance):
        rows = slice((4 - distance) * SHARD, (5 - distance) * SHARD)
        return jnp.stack([acc[0, rows, :] * SCALE, acc[1, rows, :]])

    swap_out[0] = part(1).astype(BF16)
    swap_out[1] = part(3).astype(BF16)
    send(swap_out, swap_in, send_sem.at[9], back_sem, other)
    landed(swap_in, back_sem)
    from_near = swap_in[0].astype(F32)
    from_far = swap_in[1].astype(F32)
    zero = jnp.zeros_like(from_near)
    first_core = core == 0
    far_out[1] = (part(4) + jnp.where(first_core, zero, from_far)).astype(BF16)
    send(far_out.at[1], far_in.at[1], send_sem.at[10], far_sem.at[1], along[-4])
    far_out[0] = (part(2) + jnp.where(first_core, from_far, from_near)).astype(BF16)
    send(far_out.at[0], far_in.at[0], send_sem.at[11], far_sem.at[0], along[-2])
    base = part(0) + jnp.where(first_core, from_near, zero)
    landed(far_in.at[0], far_sem.at[0])
    landed(far_in.at[1], far_sem.at[1])
    last[...] = (base + far_in[0].astype(F32) + far_in[1].astype(F32)).astype(BF16)

    def piece_of(h):
        return pl.ds(pl.multiple_of(h * PIECE, PIECE), PIECE)

    mine = columns(me, HEAD_WIDTH)
    pltpu.make_async_copy(last.at[0, piece_of(me)], dk_out.at[:, mine], dk_sem).start()
    pltpu.make_async_copy(last.at[1, piece_of(me)], dv_out.at[:, mine], dv_sem).start()
    for i in range(1, GROUPS):
        to = (c, peers[i])
        send(last.at[0, piece_of(peers[i])], dk_out.at[:, mine], send_sem.at[12], dk_sem, to)
        send(last.at[1, piece_of(peers[i])], dv_out.at[:, mine], send_sem.at[13], dv_sem, to)

    others = pl.ds(0, GROUPS - 1)
    landed(o_out, o_sem)
    landed(dq_out, dq_sem)
    landed(dk_out, dk_sem)
    landed(dv_out, dv_sem)
    landed(kv.at[:, pl.ds(0, (GROUPS - 1) * PIECE)], send_sem.at[0])
    for sem, ref in ((1, qbuf), (2, gbuf), (7, obuf), (8, dqbuf)):
        landed(ref.at[others], send_sem.at[sem])
    for sem in (3, 4, 5, 6):
        landed(kv.at[:, own], send_sem.at[sem])
    landed(swap_out, send_sem.at[9])
    landed(far_out.at[1], send_sem.at[10])
    landed(far_out.at[0], send_sem.at[11])
    landed(last.at[0, pl.ds(0, (GROUPS - 1) * PIECE)], send_sem.at[12])
    landed(last.at[1, pl.ds(0, (GROUPS - 1) * PIECE)], send_sem.at[13])


def shards(queries, keys, values, output_gradient, doc_lengths):
    hbm = pl.BlockSpec(memory_space=pl.ANY)
    dma = pltpu.SemaphoreType.DMA
    wide = (GROUPS, PIECE, COLS)
    pair = (2, 2, SHARD, HEAD_WIDTH)
    return pl.pallas_call(
        kernel,
        out_shape=[jax.ShapeDtypeStruct(a.shape, BF16) for a in (queries, queries, keys, values)],
        in_specs=[hbm] * 4 + [pl.BlockSpec(memory_space=pltpu.SMEM)],
        out_specs=[hbm] * 4,
        scratch_shapes=[
            pltpu.VMEM(wide, BF16),
            pltpu.VMEM(wide, BF16),
            pltpu.VMEM((2, WINDOW, HEAD_WIDTH), BF16),
            pltpu.VMEM((2, HEAD_WIDTH, WINDOW), BF16),
            pltpu.VMEM(wide, BF16),
            pltpu.VMEM(wide, BF16),
            pltpu.VMEM((2, WINDOW, HEAD_WIDTH), F32),
            pltpu.VMEM((REACH, ROWS), F32),
            pltpu.VMEM((REACH, ROWS), F32),
            pltpu.VMEM((REACH, ROWS), BF16),
            pltpu.VMEM(pair, BF16),
            pltpu.VMEM(pair, BF16),
            pltpu.VMEM(pair, BF16),
            pltpu.VMEM(pair, BF16),
            pltpu.VMEM((2, SHARD, HEAD_WIDTH), BF16),
            dma((GROUPS,)),
            dma((GROUPS,)),
            dma,
            dma((2,)),
            dma((2,)),
            dma,
            dma((2,)),
            dma,
            dma,
            dma,
            dma,
            dma((14,)),
        ],
        compiler_params=pltpu.CompilerParams(
            collective_id=0, has_side_effects=True, vmem_limit_bytes=50 * 2**20
        ),
    )(queries, keys, values, output_gradient, doc_lengths)


def solution(mesh):
    rows = P(("ctx", "head"), None)
    return jax.shard_map(
        shards,
        mesh=mesh,
        in_specs=(rows, rows, rows, rows, P()),
        out_specs=(rows, rows, rows, rows),
        check_vma=False,
    )
```

```python
import math

import jax
import jax.numpy as jnp
from jax import lax
from jax.experimental import pallas as pl
from jax.experimental.pallas import tpu as pltpu
from jax.sharding import PartitionSpec as P

HEAD_WIDTH = 128
DOCS = 32
SHARDS = 64
GROUPS = 8
PER_GROUP = 8
PIECE = 32
SHARD = 256
WINDOW = 1280
REACH = 1152
ROWS = PER_GROUP * PIECE
COLS = PER_GROUP * HEAD_WIDTH
SCALE = 1.0 / math.sqrt(HEAD_WIDTH)
SCALE2 = SCALE * math.log2(math.e)
MESH = pl.DeviceIdType.MESH
F32 = jnp.float32
BF16 = jnp.bfloat16


def dot_nn(a, b):
    return lax.dot_general(a, b, (((1,), (0,)), ((), ())), preferred_element_type=F32)


def dot_nt(a, b):
    return lax.dot_general(a, b, (((1,), (1,)), ((), ())), preferred_element_type=F32)


def heads_t(piece):
    rows = [piece[:, g * HEAD_WIDTH : (g + 1) * HEAD_WIDTH] for g in range(PER_GROUP)]
    return jnp.concatenate(rows, axis=0).T


def store_heads(ref, piece, which, rows):
    for g in range(PER_GROUP):
        cols = slice(g * HEAD_WIDTH, (g + 1) * HEAD_WIDTH)
        ref[piece, which, :, cols] = rows[g * PIECE : (g + 1) * PIECE]


def piece_scores(piece, shard_start, lens, qg, kv, s_buf, dp_buf):
    off = pl.multiple_of((piece // 4) * 128, 128)
    q_t = heads_t(qg[piece, 0])
    g_t = heads_t(qg[piece, 1])
    pos = shard_start + piece * PIECE + lax.rem(lax.broadcasted_iota(jnp.int32, (1, ROWS), 1), PIECE)
    start = jnp.zeros((1, ROWS), jnp.int32)
    end = jnp.int32(0)
    for n in range(DOCS):
        end = end + lens[n]
        start = jnp.where(pos >= end, end, start)
    first = shard_start - (WINDOW - SHARD) + off
    edge = REACH - 128
    s = dot_nn(kv[0, pl.ds(off, REACH), :], q_t)
    at = lax.broadcasted_iota(jnp.int32, (REACH, ROWS), 0)
    late = at >= start - first
    early_s = jnp.where(late[:edge], s[:edge], -1e30)
    last_s = jnp.where(late[edge:] & (at[edge:] <= pos - first), s[edge:], -1e30)
    s_buf[:edge, :] = early_s
    s_buf[edge:, :] = last_s
    top = jnp.maximum(jnp.max(early_s, axis=0, keepdims=True), jnp.max(last_s, axis=0, keepdims=True))
    dp_buf[...] = dot_nn(kv[1, pl.ds(off, REACH), :], g_t)
    return off, q_t, g_t, top


def piece_forward(piece, scored, kv_t, odq, s_buf, p_buf):
    off, q_t, g_t, top = scored
    p = jnp.exp2((s_buf[...] - top) * SCALE2)
    total = jnp.sum(p, axis=0, keepdims=True)
    p_b = p.astype(BF16)
    s_buf[...] = p
    p_buf[...] = p_b
    o_t = dot_nn(kv_t[1, :, pl.ds(off, REACH)], p_b)
    inv = 1.0 / total
    g_f = g_t.astype(F32)
    o_b = (o_t * inv).astype(BF16)
    delta = jnp.sum(g_f * o_b.astype(F32), axis=0, keepdims=True)
    g_n = (g_f * inv).astype(BF16)
    q_n = (q_t.astype(F32) * inv).astype(BF16)
    store_heads(odq, piece, 0, o_b.T)
    return off, inv, delta, g_n, q_n


def piece_backward(piece, done, kv_t, odq, acc, s_buf, dp_buf, p_buf):
    off, inv, delta, g_n, q_n = done
    ds = (s_buf[...] * (dp_buf[...] - delta)).astype(BF16)
    dq_t = dot_nn(kv_t[0, :, pl.ds(off, REACH)], ds)
    acc[0, pl.ds(off, REACH), :] += dot_nt(ds, q_n)
    acc[1, pl.ds(off, REACH), :] += dot_nt(p_buf[...], g_n)
    store_heads(odq, piece, 1, (dq_t * (inv * SCALE)).astype(BF16).T)


def kernel(
    q_in, k_in, v_in, g_in, lens,
    odq_out, dkv_out,
    qg_own, kv_own, qg, kv, kv_t, odq, acc, s_buf, dp_buf, p_buf,
    swap_out, swap_in, far_out, far_in, last,
    stage_sem, qg_sem, kv_sem, fwd_sem, swap_sem, back_sem, far_sem, odq_sem, dkv_sem, send_sem,
):
    c = lax.axis_index("ctx")
    me = lax.axis_index("head")
    core = lax.rem(c, 2)
    other = (c + 1 - 2 * core, me)
    ahead = (lax.rem(c + 2, SHARDS), me)
    behind = (lax.rem(c + SHARDS - 2, SHARDS), me)
    peers = [lax.rem(me + i, GROUPS) for i in range(GROUPS)]
    takers = [lax.rem(me - i + GROUPS, GROUPS) for i in range(GROUPS)]
    own = slice(WINDOW - SHARD, WINDOW)

    def columns(h, width):
        return pl.ds(pl.multiple_of(h * width, width), width)

    def rows_of(h):
        return pl.ds(pl.multiple_of(WINDOW - SHARD + h * PIECE, PIECE), PIECE)

    def back(distance):
        return pl.ds(pl.multiple_of((4 - distance) * SHARD, SHARD), SHARD)

    def local(src, dst, sem):
        pltpu.make_async_copy(src, dst, sem).start()

    def send(src, dst, sent, arrived, to):
        pltpu.make_async_remote_copy(
            src_ref=src, dst_ref=dst, send_sem=sent, recv_sem=arrived, device_id=to, device_id_type=MESH
        ).start()

    def landed(ref, sem):
        pltpu.make_async_copy(ref, ref, sem).wait()

    local(k_in, kv_own.at[0], stage_sem.at[0])
    local(v_in, kv_own.at[1], stage_sem.at[0])
    local(q_in, qg_own.at[0], stage_sem.at[1])
    local(g_in, qg_own.at[1], stage_sem.at[1])
    local(k_in.at[:, columns(me, HEAD_WIDTH)], kv.at[0, rows_of(me)], kv_sem)
    local(v_in.at[:, columns(me, HEAD_WIDTH)], kv.at[1, rows_of(me)], kv_sem)
    local(q_in.at[:, columns(me, COLS)], qg.at[me, 0], qg_sem.at[0])
    local(g_in.at[:, columns(me, COLS)], qg.at[me, 1], qg_sem.at[0])

    barrier = pltpu.get_barrier_semaphore()
    partners = [(c, peers[i]) for i in range(1, GROUPS)] + [other, ahead, behind]
    for partner in partners:
        pl.semaphore_signal(barrier, inc=1, device_id=partner, device_id_type=MESH)
    acc[...] = jnp.zeros_like(acc)
    landed(kv_own, stage_sem.at[0])
    landed(qg_own, stage_sem.at[1])
    pl.semaphore_wait(barrier, len(partners))

    for i in range(1, GROUPS):
        cols = columns(takers[i], HEAD_WIDTH)
        send(kv_own.at[:, :, cols], kv.at[:, rows_of(me)], send_sem.at[0], kv_sem, (c, takers[i]))
    for i in range(1, GROUPS):
        cols = columns(takers[i], COLS)
        send(qg_own.at[:, :, cols], qg.at[me], send_sem.at[1], qg_sem.at[i], (c, takers[i]))

    landed(kv.at[:, own], kv_sem)
    for n in range(2):
        send(kv.at[n, own], kv.at[n, back(2)], send_sem.at[2], fwd_sem.at[n], ahead)
    for n in range(2):
        kv_t[n, :, own] = kv[n, own, :].T
    for n in range(2):
        landed(kv.at[n, back(2)], fwd_sem.at[n])
        send(kv.at[n, back(2)], kv.at[n, back(4)], send_sem.at[3], fwd_sem.at[2 + n], ahead)
        send(kv.at[n, back(2 * core)], kv.at[n, back(1)], send_sem.at[4], swap_sem.at[n], other)
    for n in range(2):
        kv_t[n, :, 512:768] = kv[n, 512:768, :].T
    for n in range(2):
        landed(kv.at[n, back(1)], swap_sem.at[n])
        kv_t[n, :, 768:1024] = kv[n, 768:1024, :].T
    for n in range(2):
        landed(kv.at[n, back(4)], fwd_sem.at[2 + n])
        send(kv.at[n, back(2 * core + 2)], kv.at[n, back(3)], send_sem.at[5], swap_sem.at[2 + n], other)
    for n in range(2):
        kv_t[n, :, 0:256] = kv[n, 0:256, :].T
    for n in range(2):
        landed(kv.at[n, back(3)], swap_sem.at[2 + n])
        kv_t[n, :, 256:512] = kv[n, 256:512, :].T

    def step(i, carry):
        pair = [lax.rem(me + 2 * i + n, GROUPS) for n in range(2)]
        for n in range(2):
            landed(qg.at[pair[n]], qg_sem.at[2 * i + n])
        scored = [
            piece_scores(pair[n], c * SHARD, lens, qg, kv, s_buf.at[n], dp_buf.at[n]) for n in range(2)
        ]
        done = [piece_forward(pair[n], scored[n], kv_t, odq, s_buf.at[n], p_buf.at[n]) for n in range(2)]
        for n in range(2):
            piece_backward(pair[n], done[n], kv_t, odq, acc, s_buf.at[n], dp_buf.at[n], p_buf.at[n])
        mine = odq_out.at[:, :, columns(me, COLS)]

        @pl.when(i == 0)
        def _():
            local(odq.at[pair[0]], mine, odq_sem)

        @pl.when(i > 0)
        def _():
            send(odq.at[pair[0]], mine, send_sem.at[6], odq_sem, (c, pair[0]))

        send(odq.at[pair[1]], mine, send_sem.at[6], odq_sem, (c, pair[1]))
        return carry

    lax.fori_loop(0, GROUPS // 2, step, 0)

    def part(n, distance):
        rows = acc[n, (4 - distance) * SHARD : (5 - distance) * SHARD, :]
        return rows * SCALE if n == 0 else rows

    first_core = core == 0
    for m, distance in ((1, 3), (0, 1)):
        for n in range(2):
            swap_out[m, n] = part(n, distance).astype(BF16)
        send(swap_out.at[m], swap_in.at[m], send_sem.at[7 + m], back_sem.at[m], other)
    landed(swap_in.at[1], back_sem.at[1])
    for n in range(2):
        add = jnp.where(first_core, 0.0, swap_in[1, n].astype(F32))
        far_out[1, n] = (part(n, 4) + add).astype(BF16)
        send(far_out.at[1, n], far_in.at[1, n], send_sem.at[9], far_sem.at[n], behind)
    landed(swap_in.at[0], back_sem.at[0])
    for n in range(2):
        near = part(n, 2) + jnp.where(first_core, swap_in[1, n], swap_in[0, n]).astype(F32)
        landed(far_in.at[1, n], far_sem.at[n])
        far_out[0, n] = (near + far_in[1, n].astype(F32)).astype(BF16)
        send(far_out.at[0, n], far_in.at[0, n], send_sem.at[10], far_sem.at[2 + n], behind)
    for n in range(2):
        base = part(n, 0) + jnp.where(first_core, swap_in[0, n].astype(F32), 0.0)
        landed(far_in.at[0, n], far_sem.at[2 + n])
        last[n] = (base + far_in[0, n].astype(F32)).astype(BF16)

    def piece_of(h):
        return last.at[:, pl.ds(pl.multiple_of(h * PIECE, PIECE), PIECE)]

    mine = dkv_out.at[:, :, columns(me, HEAD_WIDTH)]
    for i in range(1, GROUPS):
        send(piece_of(peers[i]), mine, send_sem.at[11], dkv_sem, (c, peers[i]))
    local(piece_of(me), mine, dkv_sem)

    others = pl.ds(0, GROUPS - 1)
    landed(kv.at[:, pl.ds(0, (GROUPS - 1) * PIECE)], send_sem.at[0])
    landed(qg.at[others], send_sem.at[1])
    for sem in (2, 3, 4, 5):
        landed(kv.at[:, own], send_sem.at[sem])
    landed(odq.at[others], send_sem.at[6])
    landed(swap_out.at[0], send_sem.at[7])
    landed(swap_out.at[1], send_sem.at[8])
    landed(far_out.at[1], send_sem.at[9])
    landed(far_out.at[0], send_sem.at[10])
    landed(last.at[:, pl.ds(0, (GROUPS - 1) * PIECE)], send_sem.at[11])
    landed(odq_out, odq_sem)
    landed(dkv_out, dkv_sem)


def write(odq, dkv, o_out, dq_out, dk_out, dv_out, odq_buf, dkv_buf, in_sem, out_sem):
    steps = [
        (odq.at[0], odq_buf.at[0], o_out),
        (odq.at[1], odq_buf.at[1], dq_out),
        (dkv.at[0], dkv_buf.at[0], dk_out),
        (dkv.at[1], dkv_buf.at[1], dv_out),
    ]
    reads = [pltpu.make_async_copy(src, buf, in_sem.at[n]) for n, (src, buf, _) in enumerate(steps)]
    writes = [pltpu.make_async_copy(buf, dst, out_sem.at[n]) for n, (_, buf, dst) in enumerate(steps)]
    for copy in reads:
        copy.start()
    for n in range(len(steps)):
        reads[n].wait()
        writes[n].start()
    for copy in writes:
        copy.wait()


def shards(queries, keys, values, output_gradient, doc_lengths):
    hbm = pl.BlockSpec(memory_space=pl.ANY)
    dma = pltpu.SemaphoreType.DMA
    vmem = pltpu.VMEM
    wide = queries.shape
    narrow = keys.shape
    swap = (2, 2, SHARD, HEAD_WIDTH)
    odq, dkv = pl.pallas_call(
        kernel,
        out_shape=[jax.ShapeDtypeStruct((2, *wide), BF16), jax.ShapeDtypeStruct((2, *narrow), BF16)],
        in_specs=[hbm] * 4 + [pl.BlockSpec(memory_space=pltpu.SMEM)],
        out_specs=[hbm] * 2,
        scratch_shapes=[
            vmem((2, *wide), BF16),
            vmem((2, *narrow), BF16),
            vmem((GROUPS, 2, PIECE, COLS), BF16),
            vmem((2, WINDOW, HEAD_WIDTH), BF16),
            vmem((2, HEAD_WIDTH, WINDOW), BF16),
            vmem((GROUPS, 2, PIECE, COLS), BF16),
            vmem((2, WINDOW, HEAD_WIDTH), F32),
            vmem((2, REACH, ROWS), F32),
            vmem((2, REACH, ROWS), F32),
            vmem((2, REACH, ROWS), BF16),
            vmem(swap, BF16),
            vmem(swap, BF16),
            vmem(swap, BF16),
            vmem(swap, BF16),
            vmem((2, SHARD, HEAD_WIDTH), BF16),
            dma((2,)),
            dma((GROUPS,)),
            dma,
            dma((4,)),
            dma((4,)),
            dma((2,)),
            dma((4,)),
            dma,
            dma,
            dma((12,)),
        ],
        compiler_params=pltpu.CompilerParams(
            collective_id=0, has_side_effects=True, vmem_limit_bytes=63 * 2**20
        ),
    )(queries, keys, values, output_gradient, doc_lengths)
    return pl.pallas_call(
        write,
        out_shape=[jax.ShapeDtypeStruct(shape, BF16) for shape in (wide, wide, narrow, narrow)],
        in_specs=[hbm] * 2,
        out_specs=[hbm] * 4,
        scratch_shapes=[vmem((2, *wide), BF16), vmem((2, *narrow), BF16), dma((4,)), dma((4,))],
        compiler_params=pltpu.CompilerParams(vmem_limit_bytes=63 * 2**20),
    )(odq, dkv)


def solution(mesh):
    rows = P(("ctx", "head"), None)
    return jax.shard_map(
        shards,
        mesh=mesh,
        in_specs=(rows, rows, rows, rows, P()),
        out_specs=(rows, rows, rows, rows),
        check_vma=False,
    )
```

```python
import math

import jax
import jax.numpy as jnp
from jax import lax
from jax.experimental import pallas as pl
from jax.experimental.pallas import tpu as pltpu
from jax.sharding import PartitionSpec as P

HEAD_WIDTH = 128
DOCS = 32
SHARDS = 64
GROUPS = 8
PER_GROUP = 8
PIECE = 32
SHARD = 256
WINDOW = 1280
REACH = 1152
ROWS = PER_GROUP * PIECE
COLS = PER_GROUP * HEAD_WIDTH
SCALE = 1.0 / math.sqrt(HEAD_WIDTH)
SCALE2 = SCALE * math.log2(math.e)
MESH = pl.DeviceIdType.MESH
F32 = jnp.float32
BF16 = jnp.bfloat16


def dot_nn(a, b):
    return lax.dot_general(a, b, (((1,), (0,)), ((), ())), preferred_element_type=F32)


def dot_nt(a, b):
    return lax.dot_general(a, b, (((1,), (1,)), ((), ())), preferred_element_type=F32)


def heads_t(piece):
    rows = [piece[:, g * HEAD_WIDTH : (g + 1) * HEAD_WIDTH] for g in range(PER_GROUP)]
    return jnp.concatenate(rows, axis=0).T


def store_heads(ref, piece, which, rows):
    for g in range(PER_GROUP):
        cols = slice(g * HEAD_WIDTH, (g + 1) * HEAD_WIDTH)
        ref[piece, which, :, cols] = rows[g * PIECE : (g + 1) * PIECE]


def piece_scores(piece, shard_start, lens, qg, kv, s_buf, dp_buf):
    off = pl.multiple_of((piece // 4) * 128, 128)
    q_t = heads_t(qg[piece, 0])
    g_t = heads_t(qg[piece, 1])
    pos = shard_start + piece * PIECE + lax.rem(lax.broadcasted_iota(jnp.int32, (1, ROWS), 1), PIECE)
    start = jnp.zeros((1, ROWS), jnp.int32)
    end = jnp.int32(0)
    for n in range(DOCS):
        end = end + lens[n]
        start = jnp.where(pos >= end, end, start)
    first = shard_start - (WINDOW - SHARD) + off
    edge = REACH - 128
    s = dot_nn(kv[0, pl.ds(off, REACH), :], q_t)
    at = lax.broadcasted_iota(jnp.int32, (REACH, ROWS), 0)
    late = at >= start - first
    early_s = jnp.where(late[:edge], s[:edge], -1e30)
    last_s = jnp.where(late[edge:] & (at[edge:] <= pos - first), s[edge:], -1e30)
    s_buf[:edge, :] = early_s
    s_buf[edge:, :] = last_s
    top = jnp.maximum(jnp.max(early_s, axis=0, keepdims=True), jnp.max(last_s, axis=0, keepdims=True))
    dp_buf[...] = dot_nn(kv[1, pl.ds(off, REACH), :], g_t)
    return off, q_t, g_t, top


def piece_forward(piece, scored, kv_t, odq, s_buf, p_buf):
    off, q_t, g_t, top = scored
    p = jnp.exp2((s_buf[...] - top) * SCALE2)
    total = jnp.sum(p, axis=0, keepdims=True)
    p_b = p.astype(BF16)
    s_buf[...] = p
    p_buf[...] = p_b
    o_t = dot_nn(kv_t[1, :, pl.ds(off, REACH)], p_b)
    inv = 1.0 / total
    g_f = g_t.astype(F32)
    o_b = (o_t * inv).astype(BF16)
    delta = jnp.sum(g_f * o_b.astype(F32), axis=0, keepdims=True)
    g_n = (g_f * inv).astype(BF16)
    q_n = (q_t.astype(F32) * inv).astype(BF16)
    store_heads(odq, piece, 0, o_b.T)
    return off, inv, delta, g_n, q_n


def piece_backward(piece, done, kv_t, odq, acc, s_buf, dp_buf, p_buf):
    off, inv, delta, g_n, q_n = done
    ds = (s_buf[...] * (dp_buf[...] - delta)).astype(BF16)
    dq_t = dot_nn(kv_t[0, :, pl.ds(off, REACH)], ds)
    acc[0, pl.ds(off, REACH), :] += dot_nt(ds, q_n)
    acc[1, pl.ds(off, REACH), :] += dot_nt(p_buf[...], g_n)
    store_heads(odq, piece, 1, (dq_t * (inv * SCALE)).astype(BF16).T)


def kernel(
    q_in, k_in, v_in, g_in, lens,
    odq_out, dkv_out,
    qg_own, kv_own, qg, kv, kv_t, odq, acc, s_buf, dp_buf, p_buf,
    swap_out, swap_in, far_out, far_in, last,
    stage_sem, qg_sem, kv_sem, fwd_sem, swap_sem, back_sem, far_sem, odq_sem, dkv_sem, send_sem,
):
    c = lax.axis_index("ctx")
    me = lax.axis_index("head")
    core = lax.rem(c, 2)
    other = (c + 1 - 2 * core, me)
    ahead = (lax.rem(c + 2, SHARDS), me)
    behind = (lax.rem(c + SHARDS - 2, SHARDS), me)
    peers = [lax.rem(me + i, GROUPS) for i in range(GROUPS)]
    takers = [lax.rem(me - i + GROUPS, GROUPS) for i in range(GROUPS)]
    own = slice(WINDOW - SHARD, WINDOW)

    def columns(h, width):
        return pl.ds(pl.multiple_of(h * width, width), width)

    def rows_of(h):
        return pl.ds(pl.multiple_of(WINDOW - SHARD + h * PIECE, PIECE), PIECE)

    def far_rows(h):
        return pl.ds(pl.multiple_of(2 * SHARD + h * PIECE, PIECE), PIECE)

    def back(distance):
        return pl.ds(pl.multiple_of((4 - distance) * SHARD, SHARD), SHARD)

    def local(src, dst, sem):
        pltpu.make_async_copy(src, dst, sem).start()

    def send(src, dst, sent, arrived, to):
        pltpu.make_async_remote_copy(
            src_ref=src, dst_ref=dst, send_sem=sent, recv_sem=arrived, device_id=to, device_id_type=MESH
        ).start()

    def landed(ref, sem):
        pltpu.make_async_copy(ref, ref, sem).wait()

    local(k_in, kv_own.at[0], stage_sem.at[0])
    local(v_in, kv_own.at[1], stage_sem.at[0])
    local(q_in, qg_own.at[0], stage_sem.at[1])
    local(g_in, qg_own.at[1], stage_sem.at[1])
    local(k_in.at[:, columns(me, HEAD_WIDTH)], kv.at[0, rows_of(me)], kv_sem)
    local(v_in.at[:, columns(me, HEAD_WIDTH)], kv.at[1, rows_of(me)], kv_sem)
    local(q_in.at[:, columns(me, COLS)], qg.at[me, 0], qg_sem.at[0])
    local(g_in.at[:, columns(me, COLS)], qg.at[me, 1], qg_sem.at[0])

    barrier = pltpu.get_barrier_semaphore()
    partners = [(c, peers[i]) for i in range(1, GROUPS)] + [other]
    partners += [(near, h) for near in (ahead[0], behind[0]) for h in peers]
    for partner in partners:
        pl.semaphore_signal(barrier, inc=1, device_id=partner, device_id_type=MESH)
    acc[...] = jnp.zeros_like(acc)
    landed(kv_own, stage_sem.at[0])
    landed(qg_own, stage_sem.at[1])
    pl.semaphore_wait(barrier, len(partners))

    for i in range(GROUPS):
        piece = kv_own.at[:, :, columns(takers[i], HEAD_WIDTH)]
        if i > 0:
            send(piece, kv.at[:, rows_of(me)], send_sem.at[0], kv_sem, (c, takers[i]))
    for i in range(GROUPS):
        piece = kv_own.at[:, :, columns(takers[i], HEAD_WIDTH)]
        send(piece, kv.at[:, far_rows(me)], send_sem.at[2], fwd_sem.at[0], (ahead[0], takers[i]))


    def give(i):
        cols = columns(takers[i], COLS)
        send(qg_own.at[:, :, cols], qg.at[me], send_sem.at[1], qg_sem.at[i], (c, takers[i]))

    for i in range(1, 4):
        give(i)

    landed(kv.at[:, back(2)], fwd_sem.at[0])
    for n in range(2):
        send(kv.at[n, back(2)], kv.at[n, back(4)], send_sem.at[3], fwd_sem.at[2 + n], ahead)
    landed(kv.at[:, own], kv_sem)
    for n in range(2):
        send(kv.at[n, back(2 * core)], kv.at[n, back(1)], send_sem.at[4], swap_sem.at[n], other)
    for i in range(4, GROUPS):
        give(i)
    for n in range(2):
        kv_t[n, :, own] = kv[n, own, :].T
    for n in range(2):
        kv_t[n, :, 512:768] = kv[n, 512:768, :].T
    for n in range(2):
        landed(kv.at[n, back(1)], swap_sem.at[n])
        kv_t[n, :, 768:1024] = kv[n, 768:1024, :].T
    for n in range(2):
        landed(kv.at[n, back(4)], fwd_sem.at[2 + n])
        send(kv.at[n, back(2 * core + 2)], kv.at[n, back(3)], send_sem.at[5], swap_sem.at[2 + n], other)
    for n in range(2):
        kv_t[n, :, 0:256] = kv[n, 0:256, :].T
    for n in range(2):
        landed(kv.at[n, back(3)], swap_sem.at[2 + n])
        kv_t[n, :, 256:512] = kv[n, 256:512, :].T

    def step(i, carry):
        pair = [lax.rem(me + 2 * i + n, GROUPS) for n in range(2)]
        for n in range(2):
            landed(qg.at[pair[n]], qg_sem.at[2 * i + n])
        scored = [
            piece_scores(pair[n], c * SHARD, lens, qg, kv, s_buf.at[n], dp_buf.at[n]) for n in range(2)
        ]
        done = [piece_forward(pair[n], scored[n], kv_t, odq, s_buf.at[n], p_buf.at[n]) for n in range(2)]
        for n in range(2):
            piece_backward(pair[n], done[n], kv_t, odq, acc, s_buf.at[n], dp_buf.at[n], p_buf.at[n])
        mine = odq_out.at[:, :, columns(me, COLS)]

        @pl.when(i == 0)
        def _():
            local(odq.at[pair[0]], mine, odq_sem)

        @pl.when(i > 0)
        def _():
            send(odq.at[pair[0]], mine, send_sem.at[6], odq_sem, (c, pair[0]))

        send(odq.at[pair[1]], mine, send_sem.at[6], odq_sem, (c, pair[1]))
        return carry

    lax.fori_loop(0, GROUPS // 2, step, 0)

    def part(n, distance):
        rows = acc[n, (4 - distance) * SHARD : (5 - distance) * SHARD, :]
        return rows * SCALE if n == 0 else rows

    first_core = core == 0
    for m, distance in ((1, 3), (0, 1)):
        for n in range(2):
            swap_out[m, n] = part(n, distance).astype(BF16)
        send(swap_out.at[m], swap_in.at[m], send_sem.at[7 + m], back_sem.at[m], other)
    landed(swap_in.at[1], back_sem.at[1])
    for n in range(2):
        add = jnp.where(first_core, 0.0, swap_in[1, n].astype(F32))
        far_out[1, n] = (part(n, 4) + add).astype(BF16)
        send(far_out.at[1, n], far_in.at[1, n], send_sem.at[9], far_sem.at[n], behind)
    landed(swap_in.at[0], back_sem.at[0])
    for n in range(2):
        near = part(n, 2) + jnp.where(first_core, swap_in[1, n], swap_in[0, n]).astype(F32)
        landed(far_in.at[1, n], far_sem.at[n])
        far_out[0, n] = (near + far_in[1, n].astype(F32)).astype(BF16)
        send(far_out.at[0, n], far_in.at[0, n], send_sem.at[10], far_sem.at[2 + n], behind)
    for n in range(2):
        base = part(n, 0) + jnp.where(first_core, swap_in[0, n].astype(F32), 0.0)
        landed(far_in.at[0, n], far_sem.at[2 + n])
        last[n] = (base + far_in[0, n].astype(F32)).astype(BF16)

    def piece_of(h):
        return last.at[:, pl.ds(pl.multiple_of(h * PIECE, PIECE), PIECE)]

    mine = dkv_out.at[:, :, columns(me, HEAD_WIDTH)]
    for i in range(1, GROUPS):
        send(piece_of(peers[i]), mine, send_sem.at[11], dkv_sem, (c, peers[i]))
    local(piece_of(me), mine, dkv_sem)

    others = pl.ds(0, GROUPS - 1)
    landed(kv.at[:, pl.ds(0, (GROUPS - 1) * PIECE)], send_sem.at[0])
    landed(qg.at[others], send_sem.at[1])
    for sem in (2, 3, 4, 5):
        landed(kv.at[:, own], send_sem.at[sem])
    landed(odq.at[others], send_sem.at[6])
    landed(swap_out.at[0], send_sem.at[7])
    landed(swap_out.at[1], send_sem.at[8])
    landed(far_out.at[1], send_sem.at[9])
    landed(far_out.at[0], send_sem.at[10])
    landed(last.at[:, pl.ds(0, (GROUPS - 1) * PIECE)], send_sem.at[11])
    landed(odq_out, odq_sem)
    landed(dkv_out, dkv_sem)


def write(odq, dkv, o_out, dq_out, dk_out, dv_out, odq_buf, dkv_buf, in_sem, out_sem):
    steps = [
        (odq.at[0], odq_buf.at[0], o_out),
        (odq.at[1], odq_buf.at[1], dq_out),
        (dkv.at[0], dkv_buf.at[0], dk_out),
        (dkv.at[1], dkv_buf.at[1], dv_out),
    ]
    reads = [pltpu.make_async_copy(src, buf, in_sem.at[n]) for n, (src, buf, _) in enumerate(steps)]
    writes = [pltpu.make_async_copy(buf, dst, out_sem.at[n]) for n, (_, buf, dst) in enumerate(steps)]
    for copy in reads:
        copy.start()
    for n in range(len(steps)):
        reads[n].wait()
        writes[n].start()
    for copy in writes:
        copy.wait()


def shards(queries, keys, values, output_gradient, doc_lengths):
    hbm = pl.BlockSpec(memory_space=pl.ANY)
    dma = pltpu.SemaphoreType.DMA
    vmem = pltpu.VMEM
    wide = queries.shape
    narrow = keys.shape
    swap = (2, 2, SHARD, HEAD_WIDTH)
    odq, dkv = pl.pallas_call(
        kernel,
        out_shape=[jax.ShapeDtypeStruct((2, *wide), BF16), jax.ShapeDtypeStruct((2, *narrow), BF16)],
        in_specs=[hbm] * 4 + [pl.BlockSpec(memory_space=pltpu.SMEM)],
        out_specs=[hbm] * 2,
        scratch_shapes=[
            vmem((2, *wide), BF16),
            vmem((2, *narrow), BF16),
            vmem((GROUPS, 2, PIECE, COLS), BF16),
            vmem((2, WINDOW, HEAD_WIDTH), BF16),
            vmem((2, HEAD_WIDTH, WINDOW), BF16),
            vmem((GROUPS, 2, PIECE, COLS), BF16),
            vmem((2, WINDOW, HEAD_WIDTH), F32),
            vmem((2, REACH, ROWS), F32),
            vmem((2, REACH, ROWS), F32),
            vmem((2, REACH, ROWS), BF16),
            vmem(swap, BF16),
            vmem(swap, BF16),
            vmem(swap, BF16),
            vmem(swap, BF16),
            vmem((2, SHARD, HEAD_WIDTH), BF16),
            dma((2,)),
            dma((GROUPS,)),
            dma,
            dma((4,)),
            dma((4,)),
            dma((2,)),
            dma((4,)),
            dma,
            dma,
            dma((12,)),
        ],
        compiler_params=pltpu.CompilerParams(
            collective_id=0, has_side_effects=True, vmem_limit_bytes=63 * 2**20
        ),
    )(queries, keys, values, output_gradient, doc_lengths)
    return pl.pallas_call(
        write,
        out_shape=[jax.ShapeDtypeStruct(shape, BF16) for shape in (wide, wide, narrow, narrow)],
        in_specs=[hbm] * 2,
        out_specs=[hbm] * 4,
        scratch_shapes=[vmem((2, *wide), BF16), vmem((2, *narrow), BF16), dma((4,)), dma((4,))],
        compiler_params=pltpu.CompilerParams(vmem_limit_bytes=63 * 2**20),
    )(odq, dkv)


def solution(mesh):
    rows = P(("ctx", "head"), None)
    return jax.shard_map(
        shards,
        mesh=mesh,
        in_specs=(rows, rows, rows, rows, P()),
        out_specs=(rows, rows, rows, rows),
        check_vma=False,
    )
```

```python
import math

import jax
import jax.numpy as jnp
from jax import lax
from jax.experimental import pallas as pl
from jax.experimental.pallas import tpu as pltpu
from jax.sharding import PartitionSpec as P

HEAD_WIDTH = 128
DOCS = 32
SHARDS = 64
GROUPS = 8
PER_GROUP = 8
PIECE = 32
SHARD = 256
WINDOW = 1280
REACH = 1152
ROWS = PER_GROUP * PIECE
COLS = PER_GROUP * HEAD_WIDTH
SCALE = 1.0 / math.sqrt(HEAD_WIDTH)
SCALE2 = SCALE * math.log2(math.e)
MESH = pl.DeviceIdType.MESH
F32 = jnp.float32
BF16 = jnp.bfloat16


def dot_nn(a, b):
    return lax.dot_general(a, b, (((1,), (0,)), ((), ())), preferred_element_type=F32)


def dot_nt(a, b):
    return lax.dot_general(a, b, (((1,), (1,)), ((), ())), preferred_element_type=F32)


def heads_t(piece):
    rows = [piece[:, g * HEAD_WIDTH : (g + 1) * HEAD_WIDTH] for g in range(PER_GROUP)]
    return jnp.concatenate(rows, axis=0).T


def store_heads(ref, piece, which, rows):
    for g in range(PER_GROUP):
        cols = slice(g * HEAD_WIDTH, (g + 1) * HEAD_WIDTH)
        ref[piece, which, :, cols] = rows[g * PIECE : (g + 1) * PIECE]


def piece_scores(piece, shard_start, lens, qg, kv, s_buf, dp_buf):
    off = pl.multiple_of((piece // 4) * 128, 128)
    q_t = heads_t(qg[piece, 0])
    g_t = heads_t(qg[piece, 1])
    pos = shard_start + piece * PIECE + lax.rem(lax.broadcasted_iota(jnp.int32, (1, ROWS), 1), PIECE)
    start = jnp.zeros((1, ROWS), jnp.int32)
    end = jnp.int32(0)
    for n in range(DOCS):
        end = end + lens[n]
        start = jnp.where(pos >= end, end, start)
    first = shard_start - (WINDOW - SHARD) + off
    edge = REACH - 128
    s = dot_nn(kv[0, pl.ds(off, REACH), :], q_t)
    at = lax.broadcasted_iota(jnp.int32, (REACH, ROWS), 0)
    late = at >= start - first
    early_s = jnp.where(late[:edge], s[:edge], -1e30)
    last_s = jnp.where(late[edge:] & (at[edge:] <= pos - first), s[edge:], -1e30)
    s_buf[:edge, :] = early_s
    s_buf[edge:, :] = last_s
    top = jnp.maximum(jnp.max(early_s, axis=0, keepdims=True), jnp.max(last_s, axis=0, keepdims=True))
    dp_buf[...] = dot_nn(kv[1, pl.ds(off, REACH), :], g_t)
    return off, q_t, g_t, top


def piece_forward(piece, scored, kv_t, odq, s_buf, p_buf):
    off, q_t, g_t, top = scored
    p = jnp.exp2((s_buf[...] - top) * SCALE2)
    total = jnp.sum(p, axis=0, keepdims=True)
    p_b = p.astype(BF16)
    s_buf[...] = p
    p_buf[...] = p_b
    o_t = dot_nn(kv_t[1, :, pl.ds(off, REACH)], p_b)
    inv = 1.0 / total
    g_f = g_t.astype(F32)
    o_b = (o_t * inv).astype(BF16)
    delta = jnp.sum(g_f * o_b.astype(F32), axis=0, keepdims=True)
    g_n = (g_f * inv).astype(BF16)
    q_n = (q_t.astype(F32) * inv).astype(BF16)
    store_heads(odq, piece, 0, o_b.T)
    return off, inv, delta, g_n, q_n


def piece_backward(piece, done, kv_t, odq, acc, s_buf, dp_buf, p_buf):
    off, inv, delta, g_n, q_n = done
    ds = (s_buf[...] * (dp_buf[...] - delta)).astype(BF16)
    dq_t = dot_nn(kv_t[0, :, pl.ds(off, REACH)], ds)
    acc[0, pl.ds(off, REACH), :] += dot_nt(ds, q_n)
    acc[1, pl.ds(off, REACH), :] += dot_nt(p_buf[...], g_n)
    store_heads(odq, piece, 1, (dq_t * (inv * SCALE)).astype(BF16).T)


def kernel(
    q_in, k_in, v_in, g_in, lens,
    odq_out, dkv_out,
    qg_own, kv_own, qg, kv, kv_t, odq, acc, s_buf, dp_buf, p_buf,
    swap_out, swap_in, far_out, far_in, last,
    stage_sem, qg_sem, kv_sem, fwd_sem, swap_sem, back_sem, far_sem, odq_sem, dkv_sem, send_sem,
):
    c = lax.axis_index("ctx")
    me = lax.axis_index("head")
    core = lax.rem(c, 2)
    other = (c + 1 - 2 * core, me)
    ahead = (lax.rem(c + 2, SHARDS), me)
    behind = (lax.rem(c + SHARDS - 2, SHARDS), me)
    peers = [lax.rem(me + i, GROUPS) for i in range(GROUPS)]
    takers = [lax.rem(me - i + GROUPS, GROUPS) for i in range(GROUPS)]
    own = slice(WINDOW - SHARD, WINDOW)

    def columns(h, width):
        return pl.ds(pl.multiple_of(h * width, width), width)

    def rows_of(h):
        return pl.ds(pl.multiple_of(WINDOW - SHARD + h * PIECE, PIECE), PIECE)

    def far_rows(h):
        return pl.ds(pl.multiple_of(2 * SHARD + h * PIECE, PIECE), PIECE)

    def back(distance):
        return pl.ds(pl.multiple_of((4 - distance) * SHARD, SHARD), SHARD)

    def local(src, dst, sem):
        pltpu.make_async_copy(src, dst, sem).start()

    def send(src, dst, sent, arrived, to):
        pltpu.make_async_remote_copy(
            src_ref=src, dst_ref=dst, send_sem=sent, recv_sem=arrived, device_id=to, device_id_type=MESH
        ).start()

    def landed(ref, sem):
        pltpu.make_async_copy(ref, ref, sem).wait()

    local(k_in, kv_own.at[0], stage_sem.at[0])
    local(v_in, kv_own.at[1], stage_sem.at[0])
    local(q_in, qg_own.at[0], stage_sem.at[1])
    local(g_in, qg_own.at[1], stage_sem.at[1])
    local(k_in.at[:, columns(me, HEAD_WIDTH)], kv.at[0, rows_of(me)], kv_sem)
    local(v_in.at[:, columns(me, HEAD_WIDTH)], kv.at[1, rows_of(me)], kv_sem)
    local(q_in.at[:, columns(me, COLS)], qg.at[me, 0], qg_sem.at[0])
    local(g_in.at[:, columns(me, COLS)], qg.at[me, 1], qg_sem.at[0])

    barrier = pltpu.get_barrier_semaphore()
    partners = [(c, peers[i]) for i in range(1, GROUPS)] + [other]
    partners += [(near, h) for near in (ahead[0], behind[0]) for h in peers]
    for partner in partners:
        pl.semaphore_signal(barrier, inc=1, device_id=partner, device_id_type=MESH)
    acc[...] = jnp.zeros_like(acc)
    landed(kv_own, stage_sem.at[0])
    landed(qg_own, stage_sem.at[1])
    pl.semaphore_wait(barrier, len(partners))

    for i in range(GROUPS):
        piece = kv_own.at[:, :, columns(takers[i], HEAD_WIDTH)]
        if i > 0:
            send(piece, kv.at[:, rows_of(me)], send_sem.at[0], kv_sem, (c, takers[i]))
    for i in range(GROUPS):
        piece = kv_own.at[:, :, columns(takers[i], HEAD_WIDTH)]
        send(piece, kv.at[:, far_rows(me)], send_sem.at[2], fwd_sem.at[0], (ahead[0], takers[i]))


    def give(i):
        cols = columns(takers[i], COLS)
        send(qg_own.at[:, :, cols], qg.at[me], send_sem.at[1], qg_sem.at[i], (c, takers[i]))

    for i in range(1, 6):
        give(i)

    landed(kv.at[:, back(2)], fwd_sem.at[0])
    for n in range(2):
        send(kv.at[n, back(2)], kv.at[n, back(4)], send_sem.at[3], fwd_sem.at[2 + n], ahead)
    landed(kv.at[:, own], kv_sem)
    for n in range(2):
        send(kv.at[n, back(2 * core)], kv.at[n, back(1)], send_sem.at[4], swap_sem.at[n], other)
    for i in range(6, GROUPS):
        give(i)
    for n in range(2):
        kv_t[n, :, own] = kv[n, own, :].T
    for n in range(2):
        kv_t[n, :, 512:768] = kv[n, 512:768, :].T
    for n in range(2):
        landed(kv.at[n, back(1)], swap_sem.at[n])
        kv_t[n, :, 768:1024] = kv[n, 768:1024, :].T
    for n in range(2):
        landed(kv.at[n, back(4)], fwd_sem.at[2 + n])
        send(kv.at[n, back(2 * core + 2)], kv.at[n, back(3)], send_sem.at[5], swap_sem.at[2 + n], other)
    for n in range(2):
        kv_t[n, :, 0:256] = kv[n, 0:256, :].T
    for n in range(2):
        landed(kv.at[n, back(3)], swap_sem.at[2 + n])
        kv_t[n, :, 256:512] = kv[n, 256:512, :].T

    def step(i, carry):
        pair = [lax.rem(me + 2 * i + n, GROUPS) for n in range(2)]
        for n in range(2):
            landed(qg.at[pair[n]], qg_sem.at[2 * i + n])
        scored = [
            piece_scores(pair[n], c * SHARD, lens, qg, kv, s_buf.at[n], dp_buf.at[n]) for n in range(2)
        ]
        done = [piece_forward(pair[n], scored[n], kv_t, odq, s_buf.at[n], p_buf.at[n]) for n in range(2)]
        def give_back(which):
            mine = odq_out.at[which, :, columns(me, COLS)]

            @pl.when(i == 0)
            def _():
                local(odq.at[pair[0], which], mine, odq_sem)

            @pl.when(i > 0)
            def _():
                send(odq.at[pair[0], which], mine, send_sem.at[6], odq_sem, (c, pair[0]))

            send(odq.at[pair[1], which], mine, send_sem.at[6], odq_sem, (c, pair[1]))

        give_back(0)
        for n in range(2):
            piece_backward(pair[n], done[n], kv_t, odq, acc, s_buf.at[n], dp_buf.at[n], p_buf.at[n])
        give_back(1)
        return carry

    lax.fori_loop(0, GROUPS // 2, step, 0)

    def part(n, distance):
        rows = acc[n, (4 - distance) * SHARD : (5 - distance) * SHARD, :]
        return rows * SCALE if n == 0 else rows

    first_core = core == 0
    for m, distance in ((1, 3), (0, 1)):
        for n in range(2):
            swap_out[m, n] = part(n, distance).astype(BF16)
        send(swap_out.at[m], swap_in.at[m], send_sem.at[7 + m], back_sem.at[m], other)
    landed(swap_in.at[1], back_sem.at[1])
    for n in range(2):
        add = jnp.where(first_core, 0.0, swap_in[1, n].astype(F32))
        far_out[1, n] = (part(n, 4) + add).astype(BF16)
        send(far_out.at[1, n], far_in.at[1, n], send_sem.at[9], far_sem.at[n], behind)
    landed(swap_in.at[0], back_sem.at[0])
    for n in range(2):
        near = part(n, 2) + jnp.where(first_core, swap_in[1, n], swap_in[0, n]).astype(F32)
        landed(far_in.at[1, n], far_sem.at[n])
        far_out[0, n] = (near + far_in[1, n].astype(F32)).astype(BF16)
        send(far_out.at[0, n], far_in.at[0, n], send_sem.at[10], far_sem.at[2 + n], behind)
    for n in range(2):
        base = part(n, 0) + jnp.where(first_core, swap_in[0, n].astype(F32), 0.0)
        landed(far_in.at[0, n], far_sem.at[2 + n])
        last[n] = (base + far_in[0, n].astype(F32)).astype(BF16)

    def piece_of(h):
        return last.at[:, pl.ds(pl.multiple_of(h * PIECE, PIECE), PIECE)]

    mine = dkv_out.at[:, :, columns(me, HEAD_WIDTH)]
    for i in range(1, GROUPS):
        send(piece_of(peers[i]), mine, send_sem.at[11], dkv_sem, (c, peers[i]))
    local(piece_of(me), mine, dkv_sem)

    others = pl.ds(0, GROUPS - 1)
    landed(kv.at[:, pl.ds(0, (GROUPS - 1) * PIECE)], send_sem.at[0])
    landed(qg.at[others], send_sem.at[1])
    for sem in (2, 3, 4, 5):
        landed(kv.at[:, own], send_sem.at[sem])
    landed(odq.at[others], send_sem.at[6])
    landed(swap_out.at[0], send_sem.at[7])
    landed(swap_out.at[1], send_sem.at[8])
    landed(far_out.at[1], send_sem.at[9])
    landed(far_out.at[0], send_sem.at[10])
    landed(last.at[:, pl.ds(0, (GROUPS - 1) * PIECE)], send_sem.at[11])
    landed(odq_out, odq_sem)
    landed(dkv_out, dkv_sem)


def write(odq, dkv, o_out, dq_out, dk_out, dv_out, odq_buf, dkv_buf, in_sem, out_sem):
    steps = [
        (odq.at[0], odq_buf.at[0], o_out),
        (odq.at[1], odq_buf.at[1], dq_out),
        (dkv.at[0], dkv_buf.at[0], dk_out),
        (dkv.at[1], dkv_buf.at[1], dv_out),
    ]
    reads = [pltpu.make_async_copy(src, buf, in_sem.at[n]) for n, (src, buf, _) in enumerate(steps)]
    writes = [pltpu.make_async_copy(buf, dst, out_sem.at[n]) for n, (_, buf, dst) in enumerate(steps)]
    for copy in reads:
        copy.start()
    for n in range(len(steps)):
        reads[n].wait()
        writes[n].start()
    for copy in writes:
        copy.wait()


def shards(queries, keys, values, output_gradient, doc_lengths):
    hbm = pl.BlockSpec(memory_space=pl.ANY)
    dma = pltpu.SemaphoreType.DMA
    vmem = pltpu.VMEM
    wide = queries.shape
    narrow = keys.shape
    swap = (2, 2, SHARD, HEAD_WIDTH)
    odq, dkv = pl.pallas_call(
        kernel,
        out_shape=[jax.ShapeDtypeStruct((2, *wide), BF16), jax.ShapeDtypeStruct((2, *narrow), BF16)],
        in_specs=[hbm] * 4 + [pl.BlockSpec(memory_space=pltpu.SMEM)],
        out_specs=[hbm] * 2,
        scratch_shapes=[
            vmem((2, *wide), BF16),
            vmem((2, *narrow), BF16),
            vmem((GROUPS, 2, PIECE, COLS), BF16),
            vmem((2, WINDOW, HEAD_WIDTH), BF16),
            vmem((2, HEAD_WIDTH, WINDOW), BF16),
            vmem((GROUPS, 2, PIECE, COLS), BF16),
            vmem((2, WINDOW, HEAD_WIDTH), F32),
            vmem((2, REACH, ROWS), F32),
            vmem((2, REACH, ROWS), F32),
            vmem((2, REACH, ROWS), BF16),
            vmem(swap, BF16),
            vmem(swap, BF16),
            vmem(swap, BF16),
            vmem(swap, BF16),
            vmem((2, SHARD, HEAD_WIDTH), BF16),
            dma((2,)),
            dma((GROUPS,)),
            dma,
            dma((4,)),
            dma((4,)),
            dma((2,)),
            dma((4,)),
            dma,
            dma,
            dma((12,)),
        ],
        compiler_params=pltpu.CompilerParams(
            collective_id=0, has_side_effects=True, vmem_limit_bytes=63 * 2**20
        ),
    )(queries, keys, values, output_gradient, doc_lengths)
    return pl.pallas_call(
        write,
        out_shape=[jax.ShapeDtypeStruct(shape, BF16) for shape in (wide, wide, narrow, narrow)],
        in_specs=[hbm] * 2,
        out_specs=[hbm] * 4,
        scratch_shapes=[vmem((2, *wide), BF16), vmem((2, *narrow), BF16), dma((4,)), dma((4,))],
        compiler_params=pltpu.CompilerParams(vmem_limit_bytes=63 * 2**20),
    )(odq, dkv)


def solution(mesh):
    rows = P(("ctx", "head"), None)
    return jax.shard_map(
        shards,
        mesh=mesh,
        in_specs=(rows, rows, rows, rows, P()),
        out_specs=(rows, rows, rows, rows),
        check_vma=False,
    )
```

```python
import math

import jax
import jax.numpy as jnp
from jax import lax
from jax.experimental import pallas as pl
from jax.experimental.pallas import tpu as pltpu
from jax.sharding import PartitionSpec as P

HEAD_WIDTH = 128
DOCS = 32
SHARDS = 64
GROUPS = 8
PER_GROUP = 8
PIECE = 32
SHARD = 256
WINDOW = 1280
REACH = 1152
ROWS = PER_GROUP * PIECE
COLS = PER_GROUP * HEAD_WIDTH
SCALE = 1.0 / math.sqrt(HEAD_WIDTH)
SCALE2 = SCALE * math.log2(math.e)
MESH = pl.DeviceIdType.MESH
F32 = jnp.float32
BF16 = jnp.bfloat16


def dot_nn(a, b):
    return lax.dot_general(a, b, (((1,), (0,)), ((), ())), preferred_element_type=F32)


def dot_nt(a, b):
    return lax.dot_general(a, b, (((1,), (1,)), ((), ())), preferred_element_type=F32)


def heads_t(piece):
    rows = [piece[:, g * HEAD_WIDTH : (g + 1) * HEAD_WIDTH] for g in range(PER_GROUP)]
    return jnp.concatenate(rows, axis=0).T


def store_heads(ref, piece, which, rows):
    for g in range(PER_GROUP):
        cols = slice(g * HEAD_WIDTH, (g + 1) * HEAD_WIDTH)
        ref[piece, which, :, cols] = rows[g * PIECE : (g + 1) * PIECE]


def piece_scores(piece, shard_start, lens, qg, kv, s_buf, dp_buf):
    off = pl.multiple_of((piece // 4) * 128, 128)
    q_t = heads_t(qg[piece, 0])
    g_t = heads_t(qg[piece, 1])
    pos = shard_start + piece * PIECE + lax.rem(lax.broadcasted_iota(jnp.int32, (1, ROWS), 1), PIECE)
    start = jnp.zeros((1, ROWS), jnp.int32)
    end = jnp.int32(0)
    for n in range(DOCS):
        end = end + lens[n]
        start = jnp.where(pos >= end, end, start)
    first = shard_start - (WINDOW - SHARD) + off
    edge = REACH - 128
    s = dot_nn(kv[0, pl.ds(off, REACH), :], q_t)
    at = lax.broadcasted_iota(jnp.int32, (REACH, ROWS), 0)
    late = at >= start - first
    early_s = jnp.where(late[:edge], s[:edge], -1e30)
    last_s = jnp.where(late[edge:] & (at[edge:] <= pos - first), s[edge:], -1e30)
    s_buf[:edge, :] = early_s
    s_buf[edge:, :] = last_s
    top = jnp.maximum(jnp.max(early_s, axis=0, keepdims=True), jnp.max(last_s, axis=0, keepdims=True))
    dp_buf[...] = dot_nn(kv[1, pl.ds(off, REACH), :], g_t)
    return off, q_t, g_t, top


def piece_forward(piece, scored, kv_t, odq, s_buf, p_buf):
    off, q_t, g_t, top = scored
    p = jnp.exp2((s_buf[...] - top) * SCALE2)
    total = jnp.sum(p, axis=0, keepdims=True)
    p_b = p.astype(BF16)
    s_buf[...] = p
    p_buf[...] = p_b
    o_t = dot_nn(kv_t[1, :, pl.ds(off, REACH)], p_b)
    inv = 1.0 / total
    g_f = g_t.astype(F32)
    o_b = (o_t * inv).astype(BF16)
    delta = jnp.sum(g_f * o_b.astype(F32), axis=0, keepdims=True)
    g_n = (g_f * inv).astype(BF16)
    q_n = (q_t.astype(F32) * inv).astype(BF16)
    store_heads(odq, piece, 0, o_b.T)
    return off, inv, delta, g_n, q_n


def piece_backward(piece, done, kv_t, odq, acc, s_buf, dp_buf, p_buf):
    off, inv, delta, g_n, q_n = done
    ds = (s_buf[...] * (dp_buf[...] - delta)).astype(BF16)
    dq_t = dot_nn(kv_t[0, :, pl.ds(off, REACH)], ds)
    acc[0, pl.ds(off, REACH), :] += dot_nt(ds, q_n)
    acc[1, pl.ds(off, REACH), :] += dot_nt(p_buf[...], g_n)
    store_heads(odq, piece, 1, (dq_t * (inv * SCALE)).astype(BF16).T)


def kernel(
    q_in, k_in, v_in, g_in, lens,
    odq_out, dkv_out,
    qg_own, kv_own, qg, kv, kv_t, odq, acc, s_buf, dp_buf, p_buf,
    swap_out, swap_in, far_out, far_in, last,
    stage_sem, qg_sem, kv_sem, fwd_sem, swap_sem, back_sem, far_sem, odq_sem, dkv_sem, send_sem,
):
    c = lax.axis_index("ctx")
    me = lax.axis_index("head")
    core = lax.rem(c, 2)
    other = (c + 1 - 2 * core, me)
    ahead = (lax.rem(c + 2, SHARDS), me)
    behind = (lax.rem(c + SHARDS - 2, SHARDS), me)
    peers = [lax.rem(me + i, GROUPS) for i in range(GROUPS)]
    takers = [lax.rem(me - i + GROUPS, GROUPS) for i in range(GROUPS)]
    own = slice(WINDOW - SHARD, WINDOW)

    def columns(h, width):
        return pl.ds(pl.multiple_of(h * width, width), width)

    def rows_of(h):
        return pl.ds(pl.multiple_of(WINDOW - SHARD + h * PIECE, PIECE), PIECE)

    def far_rows(h):
        return pl.ds(pl.multiple_of(2 * SHARD + h * PIECE, PIECE), PIECE)

    def back(distance):
        return pl.ds(pl.multiple_of((4 - distance) * SHARD, SHARD), SHARD)

    def local(src, dst, sem):
        pltpu.make_async_copy(src, dst, sem).start()

    def send(src, dst, sent, arrived, to):
        pltpu.make_async_remote_copy(
            src_ref=src, dst_ref=dst, send_sem=sent, recv_sem=arrived, device_id=to, device_id_type=MESH
        ).start()

    def landed(ref, sem):
        pltpu.make_async_copy(ref, ref, sem).wait()

    local(k_in, kv_own.at[0], stage_sem.at[0])
    local(v_in, kv_own.at[1], stage_sem.at[0])
    local(q_in, qg_own.at[0], stage_sem.at[1])
    local(g_in, qg_own.at[1], stage_sem.at[1])
    local(k_in.at[:, columns(me, HEAD_WIDTH)], kv.at[0, rows_of(me)], kv_sem)
    local(v_in.at[:, columns(me, HEAD_WIDTH)], kv.at[1, rows_of(me)], kv_sem)
    local(q_in.at[:, columns(me, COLS)], qg.at[me, 0], qg_sem.at[0])
    local(g_in.at[:, columns(me, COLS)], qg.at[me, 1], qg_sem.at[0])

    barrier = pltpu.get_barrier_semaphore()
    partners = [(c, peers[i]) for i in range(1, GROUPS)] + [other]
    partners += [(near, h) for near in (ahead[0], behind[0]) for h in peers]
    for partner in partners:
        pl.semaphore_signal(barrier, inc=1, device_id=partner, device_id_type=MESH)
    acc[...] = jnp.zeros_like(acc)
    landed(kv_own, stage_sem.at[0])
    landed(qg_own, stage_sem.at[1])
    pl.semaphore_wait(barrier, len(partners))

    for i in range(GROUPS):
        piece = kv_own.at[:, :, columns(takers[i], HEAD_WIDTH)]
        if i > 0:
            send(piece, kv.at[:, rows_of(me)], send_sem.at[0], kv_sem, (c, takers[i]))
    for i in range(GROUPS):
        piece = kv_own.at[:, :, columns(takers[i], HEAD_WIDTH)]
        send(piece, kv.at[:, far_rows(me)], send_sem.at[2], fwd_sem.at[0], (ahead[0], takers[i]))


    def give(i):
        cols = columns(takers[i], COLS)
        send(qg_own.at[:, :, cols], qg.at[me], send_sem.at[1], qg_sem.at[i], (c, takers[i]))

    for i in range(1, 6):
        give(i)

    landed(kv.at[:, back(2)], fwd_sem.at[0])
    for n in range(2):
        send(kv.at[n, back(2)], kv.at[n, back(4)], send_sem.at[3], fwd_sem.at[2 + n], ahead)
    landed(kv.at[:, own], kv_sem)
    for n in range(2):
        send(kv.at[n, back(2 * core)], kv.at[n, back(1)], send_sem.at[4], swap_sem.at[n], other)
    for i in range(6, GROUPS):
        give(i)
    for n in range(2):
        kv_t[n, :, own] = kv[n, own, :].T
    for n in range(2):
        kv_t[n, :, 512:768] = kv[n, 512:768, :].T
    for n in range(2):
        landed(kv.at[n, back(1)], swap_sem.at[n])
        kv_t[n, :, 768:1024] = kv[n, 768:1024, :].T
    for n in range(2):
        landed(kv.at[n, back(4)], fwd_sem.at[2 + n])
        send(kv.at[n, back(2 * core + 2)], kv.at[n, back(3)], send_sem.at[5], swap_sem.at[2 + n], other)
    for n in range(2):
        kv_t[n, :, 0:256] = kv[n, 0:256, :].T
    for n in range(2):
        landed(kv.at[n, back(3)], swap_sem.at[2 + n])
        kv_t[n, :, 256:512] = kv[n, 256:512, :].T

    def step(i, carry):
        pair = [lax.rem(me + 2 * i + n, GROUPS) for n in range(2)]
        for n in range(2):
            landed(qg.at[pair[n]], qg_sem.at[2 * i + n])
        scored = [
            piece_scores(pair[n], c * SHARD, lens, qg, kv, s_buf.at[n], dp_buf.at[n]) for n in range(2)
        ]
        done = [piece_forward(pair[n], scored[n], kv_t, odq, s_buf.at[n], p_buf.at[n]) for n in range(2)]
        def give_back(which):
            mine = odq_out.at[which, :, columns(me, COLS)]

            @pl.when(i == 0)
            def _():
                local(odq.at[pair[0], which], mine, odq_sem)

            @pl.when(i > 0)
            def _():
                send(odq.at[pair[0], which], mine, send_sem.at[6], odq_sem, (c, pair[0]))

            send(odq.at[pair[1], which], mine, send_sem.at[6], odq_sem, (c, pair[1]))

        give_back(0)
        for n in range(2):
            piece_backward(pair[n], done[n], kv_t, odq, acc, s_buf.at[n], dp_buf.at[n], p_buf.at[n])
        give_back(1)
        return carry

    lax.fori_loop(0, GROUPS // 2, step, 0)

    def part(n, distance):
        rows = acc[n, (4 - distance) * SHARD : (5 - distance) * SHARD, :]
        return rows * SCALE if n == 0 else rows

    first_core = core == 0
    for m, distance in ((1, 3), (0, 1)):
        for n in range(2):
            swap_out[m, n] = part(n, distance).astype(BF16)
        send(swap_out.at[m], swap_in.at[m], send_sem.at[7 + m], back_sem.at[m], other)
    landed(swap_in.at[1], back_sem.at[1])
    for n in range(2):
        add = jnp.where(first_core, 0.0, swap_in[1, n].astype(F32))
        far_out[1, n] = (part(n, 4) + add).astype(BF16)
        send(far_out.at[1, n], far_in.at[1, n], send_sem.at[9], far_sem.at[n], behind)
    landed(swap_in.at[0], back_sem.at[0])
    for n in range(2):
        near = part(n, 2) + jnp.where(first_core, swap_in[1, n], swap_in[0, n]).astype(F32)
        landed(far_in.at[1, n], far_sem.at[n])
        far_out[0, n] = (near + far_in[1, n].astype(F32)).astype(BF16)
        send(far_out.at[0, n], far_in.at[0, n], send_sem.at[10], far_sem.at[2 + n], behind)
    for n in range(2):
        base = part(n, 0) + jnp.where(first_core, swap_in[0, n].astype(F32), 0.0)
        landed(far_in.at[0, n], far_sem.at[2 + n])
        last[n] = (base + far_in[0, n].astype(F32)).astype(BF16)
        mine = dkv_out.at[n, :, columns(me, HEAD_WIDTH)]
        for i, h in enumerate(peers):
            piece = last.at[n, pl.ds(pl.multiple_of(h * PIECE, PIECE), PIECE)]
            if i > 0:
                send(piece, mine, send_sem.at[11], dkv_sem, (c, h))
            else:
                local(piece, mine, dkv_sem)

    others = pl.ds(0, GROUPS - 1)
    landed(kv.at[:, pl.ds(0, (GROUPS - 1) * PIECE)], send_sem.at[0])
    landed(qg.at[others], send_sem.at[1])
    for sem in (2, 3, 4, 5):
        landed(kv.at[:, own], send_sem.at[sem])
    landed(odq.at[others], send_sem.at[6])
    landed(swap_out.at[0], send_sem.at[7])
    landed(swap_out.at[1], send_sem.at[8])
    landed(far_out.at[1], send_sem.at[9])
    landed(far_out.at[0], send_sem.at[10])
    landed(last.at[:, pl.ds(0, (GROUPS - 1) * PIECE)], send_sem.at[11])
    landed(odq_out, odq_sem)
    landed(dkv_out, dkv_sem)


def write(odq, dkv, o_out, dq_out, dk_out, dv_out, odq_buf, dkv_buf, in_sem, out_sem):
    steps = [
        (odq.at[0], odq_buf.at[0], o_out),
        (odq.at[1], odq_buf.at[1], dq_out),
        (dkv.at[0], dkv_buf.at[0], dk_out),
        (dkv.at[1], dkv_buf.at[1], dv_out),
    ]
    reads = [pltpu.make_async_copy(src, buf, in_sem.at[n]) for n, (src, buf, _) in enumerate(steps)]
    writes = [pltpu.make_async_copy(buf, dst, out_sem.at[n]) for n, (_, buf, dst) in enumerate(steps)]
    for copy in reads:
        copy.start()
    for n in range(len(steps)):
        reads[n].wait()
        writes[n].start()
    for copy in writes:
        copy.wait()


def shards(queries, keys, values, output_gradient, doc_lengths):
    hbm = pl.BlockSpec(memory_space=pl.ANY)
    dma = pltpu.SemaphoreType.DMA
    vmem = pltpu.VMEM
    wide = queries.shape
    narrow = keys.shape
    swap = (2, 2, SHARD, HEAD_WIDTH)
    odq, dkv = pl.pallas_call(
        kernel,
        out_shape=[jax.ShapeDtypeStruct((2, *wide), BF16), jax.ShapeDtypeStruct((2, *narrow), BF16)],
        in_specs=[hbm] * 4 + [pl.BlockSpec(memory_space=pltpu.SMEM)],
        out_specs=[hbm] * 2,
        scratch_shapes=[
            vmem((2, *wide), BF16),
            vmem((2, *narrow), BF16),
            vmem((GROUPS, 2, PIECE, COLS), BF16),
            vmem((2, WINDOW, HEAD_WIDTH), BF16),
            vmem((2, HEAD_WIDTH, WINDOW), BF16),
            vmem((GROUPS, 2, PIECE, COLS), BF16),
            vmem((2, WINDOW, HEAD_WIDTH), F32),
            vmem((2, REACH, ROWS), F32),
            vmem((2, REACH, ROWS), F32),
            vmem((2, REACH, ROWS), BF16),
            vmem(swap, BF16),
            vmem(swap, BF16),
            vmem(swap, BF16),
            vmem(swap, BF16),
            vmem((2, SHARD, HEAD_WIDTH), BF16),
            dma((2,)),
            dma((GROUPS,)),
            dma,
            dma((4,)),
            dma((4,)),
            dma((2,)),
            dma((4,)),
            dma,
            dma,
            dma((12,)),
        ],
        compiler_params=pltpu.CompilerParams(
            collective_id=0, has_side_effects=True, vmem_limit_bytes=63 * 2**20
        ),
    )(queries, keys, values, output_gradient, doc_lengths)
    return pl.pallas_call(
        write,
        out_shape=[jax.ShapeDtypeStruct(shape, BF16) for shape in (wide, wide, narrow, narrow)],
        in_specs=[hbm] * 2,
        out_specs=[hbm] * 4,
        scratch_shapes=[vmem((2, *wide), BF16), vmem((2, *narrow), BF16), dma((4,)), dma((4,))],
        compiler_params=pltpu.CompilerParams(vmem_limit_bytes=63 * 2**20),
    )(odq, dkv)


def solution(mesh):
    rows = P(("ctx", "head"), None)
    return jax.shard_map(
        shards,
        mesh=mesh,
        in_specs=(rows, rows, rows, rows, P()),
        out_specs=(rows, rows, rows, rows),
        check_vma=False,
    )
```
